512 devices in a mesh: chan: 32 (over z, y_lo), row: 2 (over core), col: 8 (over x, y_hi).
Axes of the slice: x: 4, y: 4 (y_hi: 2, y_lo: 2; y = y_hi * 2 + y_lo), z: 16, core: 2. Of those that a mesh axis runs over, the one named last changes fastest.
Arguments:
- volts: bfloat16 [2, 1024, 2, 52736], P(None, ('chan', 'row', 'col')), may hold values from -6 to 6
- taps: float32 [8, 512], replicated, may hold values from -2 to 2
- owner_map: int32 [384], replicated, may hold values from 0 to 255, as said below
- assign: int32 [512], replicated, may hold values from 0 to 511, each once
Outputs:
- visibility: bfloat16 [512, 2, 1024, 1024], P(('chan', 'col'), None, 'row')
The draws below stay inside these ranges and needn't reach their ends.
Inputs may be any that keep to these rules, and one draw needn't show every extreme that they name: `owner_map`: each owner holds 1 to 2 channels, and some owner holds exactly 2. `assign`: A permutation of the stations.
All inputs are finite; a program needn't handle non-finite values.
Results may differ from the reference program's by a relative error of at most 0.0055.
Values may be sent and summed in bfloat16 or wider, within the bound.
A program may use at most 64 MiB of HBM per device.

```python
import math
import jax
import jax.numpy as jnp
from jax import lax

STATIONS = 512
NFFT = 512
TAPS = 8
BATCHES = 2
SPEC_B = 96
CAP = 2
INPUTS = 1024
SAMPLES = 52736
OWNERS = 256
NCHAN = 384


def draw_owner_map(key, part):
    pair_count = OWNERS // 2
    key_flips, key_owner, key_channel = jax.random.split(jax.random.fold_in(key, 7), 3)
    flips = jax.random.randint(key_flips, (pair_count,), 0, 2)
    sizes = jnp.stack([1 + flips * (CAP - 1), CAP - flips * (CAP - 1)], axis=1).reshape(OWNERS)
    sizes = jnp.take(sizes, jax.random.permutation(key_owner, OWNERS), axis=0)
    bounds = jnp.cumsum(sizes)
    places = jnp.arange(NCHAN)
    sorted_owner = jnp.sum((bounds[None, :] <= places[:, None]).astype(jnp.int32), axis=1)
    shuffle = jax.random.permutation(key_channel, NCHAN)
    return jnp.take(sorted_owner, shuffle, axis=0).astype(jnp.int32)


def shard_levels(rng, extent, cuts, low, top_value):
    loudness = 1.0
    for dim, parts in cuts:
        steps = jax.random.uniform(jax.random.fold_in(jax.random.fold_in(rng, 6), dim), (parts,), jnp.float32, low / len(cuts), top_value / len(cuts))
        loudness = loudness * jnp.repeat(jnp.exp(steps), extent[dim] // parts).reshape((-1,) + (1,) * (len(extent) - 1 - dim))
    return loudness


def centred(rng, extent, spread, most, cuts=(), kind=jnp.bfloat16):
    level = shard_levels(rng, extent, cuts, -0.22, 0.18) if cuts else 1.0
    entries = jax.random.normal(rng, extent, jnp.float32) * spread * level
    return jnp.minimum(jnp.maximum(entries, -most), most).astype(kind)


def setup_inputs(seed: int = 0) -> dict:
    seeds = jax.random.split(jax.random.key(seed), 5)
    volts = centred(seeds[0], (BATCHES, INPUTS, 2, SAMPLES), 1.0, 6.0, ((1, 512),))
    taps = centred(seeds[1], (TAPS, NFFT), TAPS ** -0.5, 2.0, (), jnp.float32)
    owner_map = draw_owner_map(jax.random.fold_in(seeds[4], 71), 0)
    assign = jax.random.permutation(seeds[3], STATIONS).astype(jnp.int32)
    return dict(volts=volts, taps=taps, owner_map=owner_map, assign=assign)


def slot_table(owner_map, owner_count, slot_count):
    channel_count = owner_map.shape[0]
    ranking = jnp.argsort(owner_map * channel_count + jnp.arange(channel_count, dtype=jnp.int32)).astype(jnp.int32)
    counts = lax.optimization_barrier(jnp.sum((owner_map[None, :] == jnp.arange(owner_count, dtype=jnp.int32)[:, None]).astype(jnp.int32), axis=1))
    starts = jnp.cumsum(counts) - counts
    slot_index = jnp.arange(slot_count, dtype=jnp.int32)
    position = jnp.clip(starts[:, None] + slot_index[None, :], 0, channel_count - 1).astype(jnp.int32)
    channel = jnp.take(ranking, position, axis=0)
    is_live = slot_index[None, :] < counts[:, None]
    return (channel, is_live)

def filter_bank(volts_batch, taps):
    count = volts_batch.shape[0]
    signal = volts_batch.astype(jnp.float32).reshape(count, 2, SPEC_B + TAPS - 1, NFFT)
    summed = jnp.zeros((count, 2, SPEC_B, NFFT), jnp.float32)
    for tap_index in range(TAPS):
        summed = summed + taps[tap_index][None, None, None, :] * signal[:, :, tap_index:tap_index + SPEC_B, :]
    return summed

def reference(volts, taps, owner_map, assign):
    points = jnp.arange(NFFT, dtype=jnp.int32)
    channels = jnp.arange(NCHAN, dtype=jnp.int32)
    phase = (points[:, None] * channels[None, :] % NFFT).astype(jnp.float32) * (2.0 * math.pi / NFFT)
    unit = 1.0 / math.sqrt(NFFT)
    cosine = jnp.cos(phase) * unit
    sine = jnp.sin(phase) * unit
    high = lax.Precision.HIGHEST
    spectra_list = []
    for batch in range(BATCHES):
        summed = filter_bank(volts[batch], taps)
        real_in = summed[:, 0]
        imag_in = summed[:, 1]
        real_out = jnp.einsum('isj,jk->iks', real_in, cosine, precision=high) + jnp.einsum('isj,jk->iks', imag_in, sine, precision=high)
        imag_out = jnp.einsum('isj,jk->iks', imag_in, cosine, precision=high) - jnp.einsum('isj,jk->iks', real_in, sine, precision=high)
        spectra_list.append(jnp.concatenate([real_out, imag_out], axis=2).astype(jnp.bfloat16))
    spectra = jnp.stack(spectra_list, 0)
    channel, is_live = slot_table(owner_map, OWNERS, CAP)
    positions = jnp.arange(INPUTS, dtype=jnp.int32)
    pick = (2 * jnp.take(assign, positions // 2, axis=0) + positions % 2).astype(jnp.int32)
    scale = 1.0 / math.sqrt(2 * BATCHES * SPEC_B)

    def one_slot(entry):
        slot_channel, slot_live = entry
        total = jnp.zeros((2 * INPUTS, INPUTS), jnp.float32)
        for batch in range(BATCHES):
            chosen = jnp.take(spectra[batch], slot_channel, axis=1)
            ordered = jnp.take(chosen, pick, axis=0)
            flipped = jnp.concatenate([ordered[:, SPEC_B:], -ordered[:, :SPEC_B]], axis=1)
            stacked = jnp.concatenate([ordered, flipped], axis=0)
            total = total + jnp.dot(stacked, ordered.T, preferred_element_type=jnp.float32)
        total = jnp.where(slot_live, total, jnp.zeros_like(total)) * scale
        return total.reshape(2, INPUTS, INPUTS).astype(jnp.bfloat16)
    return lax.map(one_slot, (channel.reshape(-1), is_live.reshape(-1)))
```

```python
import functools
import math

import jax
import jax.numpy as jnp
import ml_dtypes
import numpy as np
from jax import lax
from jax.experimental import pallas as pl
from jax.experimental.pallas import tpu as pltpu
from jax.sharding import PartitionSpec as P

NFFT = 512
TAPS = 8
BATCHES = 2
SPEC_B = 96
NCHAN = 384
BLOCKS = SPEC_B + TAPS - 1
SPEC = BATCHES * SPEC_B
WIDTH = 2 * SPEC
MESH = pl.DeviceIdType.MESH


def dft_tables():
    phase = 2.0 * np.pi / NFFT * (np.outer(np.arange(NCHAN), np.arange(NFFT)) % NFFT)
    both = np.stack([np.cos(phase), np.sin(phase)], axis=1) / math.sqrt(NFFT)
    both = both.reshape(NCHAN, 2, 4, 128).transpose(0, 2, 1, 3).reshape(NCHAN, 2 * NFFT)
    high = both.astype(np.float32).astype(ml_dtypes.bfloat16)
    low = (both - high.astype(np.float64)).astype(np.float32).astype(ml_dtypes.bfloat16)
    return high, low


def rows_by(left, right):
    return lax.dot_general(
        left, right, (((1,), (1,)), ((), ())), preferred_element_type=jnp.float32
    )


def times(left, right):
    return jnp.dot(left, right, preferred_element_type=jnp.float32)


def one_hot(found):
    return jnp.where(found, 1.0, 0.0).astype(jnp.bfloat16)


def exchange_kernel(
    volts, taps, owner, assign, table_hi, table_lo, out,
    vbuf, tap_v, tapx, own_v, asg_v, thi, tlo, filt, ghi, glo, wsel, perm, hot_a, hot_b,
    send_a, send_b, recv_a, recv_b, stage_a, stage_b, x_a, x_b, spread,
    lsem, za_s, za_r, xb_s, xb_r, zb_s, zb_r, xa_s, xa_r, fa_s, fa_r, fb_s, fb_r,
):
    chan, row, col = lax.axis_index("chan"), lax.axis_index("row"), lax.axis_index("col")
    z, o = chan // 2, chan % 2 * 8 + col

    def device(zz, oo, rr):
        return (zz * 2 + oo // 8, rr, oo % 8)

    def later(base, step):
        return lax.rem(base + step, 16)

    barrier = pltpu.get_barrier_semaphore()

    def greet(d, carry):
        pl.semaphore_signal(barrier, inc=1, device_id=device(later(z, d), o, row), device_id_type=MESH)
        pl.semaphore_signal(barrier, inc=1, device_id=device(z, later(o, d), row), device_id_type=MESH)
        return carry

    lax.fori_loop(1, 16, greet, 0)
    pl.semaphore_signal(barrier, inc=1, device_id=device(z, o, 1 - row), device_id_type=MESH)

    loads = [
        pltpu.make_async_copy(volts.at[:, 0], vbuf.at[0], lsem.at[0]),
        pltpu.make_async_copy(volts.at[:, 1], vbuf.at[1], lsem.at[1]),
        pltpu.make_async_copy(taps, tap_v, lsem.at[2]),
        pltpu.make_async_copy(owner, own_v, lsem.at[3]),
        pltpu.make_async_copy(assign, asg_v, lsem.at[4]),
        pltpu.make_async_copy(table_hi, thi, lsem.at[5]),
        pltpu.make_async_copy(table_lo, tlo, lsem.at[6]),
    ]
    for k in (3, 2, 0, 5, 6, 1, 4):
        loads[k].start()

    def far(i):
        return 8 + (1 - 2 * lax.rem(i, 2)) * ((i + 1) // 2)

    def copy_za(d):
        t = later(z, d)
        return pltpu.make_async_remote_copy(
            send_a.at[t], recv_a.at[z], za_s.at[d], za_r.at[d], device_id=device(t, o, row), device_id_type=MESH)

    def copy_xb(d):
        t = later(o, d)
        return pltpu.make_async_remote_copy(
            send_b.at[t], recv_b.at[o], xb_s.at[d], xb_r.at[d], device_id=device(z, t, row), device_id_type=MESH)

    def copy_zb(d):
        t = later(z, d)
        return pltpu.make_async_remote_copy(
            stage_b.at[t], x_b.at[row * 16 + z], zb_s.at[d], zb_r.at[d], device_id=device(t, o, row), device_id_type=MESH)

    def copy_xa(d):
        t = later(o, d)
        return pltpu.make_async_remote_copy(
            stage_a.at[t], x_a.at[row * 16 + o], xa_s.at[d], xa_r.at[d], device_id=device(z, t, row), device_id_type=MESH)

    def forward_a():
        half = pl.ds(row * 16, 16)
        return pltpu.make_async_remote_copy(
            x_a.at[half], x_a.at[half], fa_s, fa_r, device_id=device(z, o, 1 - row), device_id_type=MESH)

    def forward_b(block):
        return pltpu.make_async_remote_copy(
            x_b.at[row * 16 + block], x_b.at[row * 16 + block], fb_s.at[block], fb_r.at[block],
            device_id=device(z, o, 1 - row), device_id_type=MESH)

    def each(action):
        def step(i, carry):
            action(far(i))
            return carry

        lax.fori_loop(0, 15, step, 0)

    def choose(swapped):
        line = lax.broadcasted_iota(jnp.int32, (256, NCHAN), 0)
        owner_of_line = (line % 16) * 16 + line // 16 if swapped else line
        owned = jnp.where(own_v[...].reshape(1, NCHAN) == owner_of_line, 1.0, 0.0)
        before = jnp.where(
            lax.broadcasted_iota(jnp.int32, (NCHAN, NCHAN), 0)
            < lax.broadcasted_iota(jnp.int32, (NCHAN, NCHAN), 1), 1.0, 0.0).astype(jnp.bfloat16)
        earlier = times(owned.astype(jnp.bfloat16), before)
        for slot in range(2):
            taken = jnp.where(earlier == float(slot), owned, 0.0).astype(jnp.bfloat16)
            wsel[:, slot * 16 : slot * 16 + 16, :] = taken.reshape(16, 16, NCHAN)

    def spectra(pol):
        loads[pol].wait()
        if pol == 0:
            loads[2].wait()
            for m in range(TAPS):
                for j in range(4):
                    line = tap_v[m : m + 1, j * 128 : j * 128 + 128]
                    tapx[m, 2 * j : 2 * j + 2, :] = jnp.broadcast_to(line, (2, 128))
        weights = [tapx[m] for m in range(TAPS)]

        def chunk(i, carry):
            first = i * 8
            for b in range(BATCHES):
                signal = [vbuf[pol, b, first + t].astype(jnp.float32) for t in range(15)]
                for s in range(8):
                    total = weights[0] * signal[s]
                    for m in range(1, TAPS):
                        total = total + weights[m] * signal[s + m]
                    filt[pl.ds(pl.multiple_of((b * SPEC_B + first + s) * 8, 8), 8), :] = total
            return carry

        lax.fori_loop(0, SPEC_B // 8, chunk, 0)
        for q in range(8):
            value = filt[pl.ds(q, SPEC, stride=8), :]
            high = value.astype(jnp.bfloat16)
            low = (value - high.astype(jnp.float32)).astype(jnp.bfloat16)
            here = slice(q * 128, q * 128 + 128)
            other = slice((q ^ 1) * 128, (q ^ 1) * 128 + 128)
            for held, part in ((ghi, high), (glo, low)):
                held[:SPEC, here] = part
                held[SPEC:, other] = part if q % 2 else -part
        if pol == 0:
            loads[5].wait()
            loads[6].wait()
        total = rows_by(thi[...], ghi[...]) + (rows_by(tlo[...], ghi[...]) + rows_by(thi[...], glo[...]))
        return total.astype(jnp.bfloat16)

    def chosen(pol):
        picked = times(wsel[...].reshape(512, NCHAN), spectra(pol))
        return picked.astype(jnp.bfloat16).reshape(16, 32, WIDTH)

    def regroup(ref):
        return times(perm[...], ref[...].reshape(512, WIDTH)).astype(jnp.bfloat16).reshape(16, 32, WIDTH)

    loads[3].wait()
    choose(False)
    send_a[...] = chosen(0)
    pl.semaphore_wait(barrier, 31)
    each(lambda d: copy_za(d).start())
    recv_a[z] = send_a[z]

    choose(True)
    send_b[...] = chosen(1)
    each(lambda d: copy_xb(d).start())
    recv_b[o] = send_b[o]

    to = lax.broadcasted_iota(jnp.int32, (512, 512), 0)
    perm[...] = one_hot(
        (to % 16) * 32 + (to // 16 % 2) * 16 + to // 32 == lax.broadcasted_iota(jnp.int32, (512, 512), 1))
    loads[4].wait()
    placed = jnp.broadcast_to(asg_v[...], (128, 512)).T
    for t in range(4):
        k = lax.broadcasted_iota(jnp.int32, (512, 128), 1) + t * 128
        r, up, low = k // 256, k // 16 % 16, k % 16
        hot_a[:, t * 128 : t * 128 + 128] = one_hot(placed == low * 32 + up // 8 * 16 + r * 8 + up % 8)
        hot_b[:, t * 128 : t * 128 + 128] = one_hot(placed == up * 32 + low // 8 * 16 + r * 8 + low % 8)

    def ordered(hot, held, pol):
        for slot in range(2):
            lines = held[:, slot * 16 : slot * 16 + 16, :].reshape(512, WIDTH)
            value = times(hot[...], lines)
            for t in range(3):
                spread[slot, t, pl.ds(pol, 512, stride=2), :] = value[:, t * 128 : t * 128 + 128]

    each(lambda d: copy_xb(d).wait_recv())
    stage_b[...] = regroup(recv_b)
    each(lambda d: copy_zb(d).start())
    x_b[row * 16 + z] = stage_b[z]
    forward_b(z).start()

    each(lambda d: copy_za(d).wait_recv())
    stage_a[...] = regroup(recv_a)
    each(lambda d: copy_xa(d).start())
    x_a[row * 16 + o] = stage_a[o]

    each(lambda d: copy_xa(d).wait_recv())
    forward_a().start()

    def pass_on(i, carry):
        d = far(i)
        copy_zb(d).wait_recv()
        forward_b(later(z, 16 - d)).start()
        return carry

    forward_a().wait_recv()
    ordered(hot_a, x_a, 0)
    lax.fori_loop(0, 15, pass_on, 0)

    def arrived(block, carry):
        forward_b(block).wait_recv()
        return carry

    lax.fori_loop(0, 16, arrived, 0)
    ordered(hot_b, x_b, 1)
    for slot in range(2):
        for t in range(3):
            out[slot, :, t * 128 : t * 128 + 128] = spread[slot, t].astype(jnp.bfloat16)

    each(lambda d: copy_za(d).wait_send())
    each(lambda d: copy_xb(d).wait_send())
    each(lambda d: copy_zb(d).wait_send())
    each(lambda d: copy_xa(d).wait_send())
    forward_a().wait_send()

    def left(block, carry):
        forward_b(block).wait_send()
        return carry

    lax.fori_loop(0, 16, left, 0)


def exchange(volts, taps, owner_map, assign):
    high, low = dft_tables()
    held = lambda *shape: pltpu.VMEM(shape, jnp.bfloat16)
    dma = pltpu.SemaphoreType.DMA
    block = (16, 32, WIDTH)
    return pl.pallas_call(
        exchange_kernel,
        out_shape=jax.ShapeDtypeStruct((2, 1024, WIDTH), jnp.bfloat16),
        in_specs=[pl.BlockSpec(memory_space=pl.ANY)] * 6,
        out_specs=pl.BlockSpec(memory_space=pltpu.VMEM),
        scratch_shapes=[
            held(2, BATCHES, BLOCKS, 8, 128),
            pltpu.VMEM((TAPS, NFFT), jnp.float32),
            pltpu.VMEM((TAPS, 8, 128), jnp.float32),
            pltpu.VMEM((NCHAN,), jnp.int32),
            pltpu.VMEM((1, 512), jnp.int32),
            held(NCHAN, 2 * NFFT),
            held(NCHAN, 2 * NFFT),
            pltpu.VMEM((SPEC * 8, 128), jnp.float32),
            held(WIDTH, 2 * NFFT),
            held(WIDTH, 2 * NFFT),
            held(16, 32, NCHAN),
            held(512, 512),
            held(512, 512),
            held(512, 512),
            held(*block),
            held(*block),
            held(*block),
            held(*block),
            held(*block),
            held(*block),
            held(32, 32, WIDTH),
            held(32, 32, WIDTH),
            pltpu.VMEM((2, 3, 1024, 128), jnp.float32),
            dma((7,)),
            dma((16,)), dma((16,)), dma((16,)), dma((16,)), dma((16,)), dma((16,)), dma((16,)), dma((16,)),
            dma, dma, dma((16,)), dma((16,)),
        ],
        compiler_params=pltpu.CompilerParams(
            collective_id=0, has_side_effects=True, vmem_limit_bytes=61 << 20
        ),
        name="exchange",
    )(volts, taps, owner_map, assign, jnp.asarray(high), jnp.asarray(low))


def visibility_kernel(lines, out, mine, turned):
    half = lax.axis_index("row") * 512

    @pl.when(pl.program_id(1) == 0)
    def _():
        ours = lines[0, pl.ds(pl.multiple_of(half, 512), 512), :].astype(jnp.float32)
        first = lax.broadcasted_iota(jnp.int32, (512, WIDTH), 1) < SPEC
        rolled = pltpu.roll(ours, SPEC, 1)
        mine[...] = ours.astype(jnp.bfloat16)
        turned[...] = jnp.where(first, rolled, -rolled).astype(jnp.bfloat16)

    scale = 1.0 / math.sqrt(WIDTH)
    width = out.shape[3]
    across = lines[0, pl.ds(pl.multiple_of(pl.program_id(1) * width, width), width), :]
    out[0, 0] = (rows_by(mine[...], across) * scale).astype(jnp.bfloat16)
    out[0, 1] = (rows_by(turned[...], across) * scale).astype(jnp.bfloat16)


def visibilities(lines):
    width = 256
    return pl.pallas_call(
        visibility_kernel,
        grid=(2, 1024 // width),
        out_shape=jax.ShapeDtypeStruct((2, 2, 512, 1024), jnp.bfloat16),
        in_specs=[pl.BlockSpec((1, 1024, WIDTH), lambda slot, j: (slot, 0, 0))],
        out_specs=pl.BlockSpec((1, 2, 512, width), lambda slot, j: (slot, 0, 0, j)),
        scratch_shapes=[pltpu.VMEM((512, WIDTH), jnp.bfloat16)] * 2,
        compiler_params=pltpu.CompilerParams(vmem_limit_bytes=61 << 20),
        name="visibilities",
    )(lines)


def shards(volts, taps, owner_map, assign):
    blocks = volts.reshape(BATCHES, 2, 2, BLOCKS, 4, 128).transpose(0, 1, 3, 4, 2, 5)
    lines = exchange(
        blocks.reshape(BATCHES, 2, BLOCKS, 8, 128),
        taps,
        owner_map,
        assign.reshape(1, 512),
    )
    return visibilities(lines)


def solution(mesh):
    placed = (P(None, ("chan", "row", "col"), None, None), P(), P(), P())
    return jax.shard_map(
        shards,
        mesh=mesh,
        in_specs=placed,
        out_specs=P(("chan", "col"), None, "row", None),
        check_vma=False,
    )
```

```python
import functools
import math

import jax
import jax.numpy as jnp
import ml_dtypes
import numpy as np
from jax import lax
from jax.experimental import pallas as pl
from jax.experimental.pallas import tpu as pltpu
from jax.sharding import PartitionSpec as P

NFFT = 512
TAPS = 8
BATCHES = 2
SPEC_B = 96
NCHAN = 384
BLOCKS = SPEC_B + TAPS - 1
SPEC = BATCHES * SPEC_B
WIDTH = 2 * SPEC
MESH = pl.DeviceIdType.MESH


def dft_tables():
    phase = 2.0 * np.pi / NFFT * (np.outer(np.arange(NCHAN), np.arange(NFFT)) % NFFT)
    both = np.stack([np.cos(phase), np.sin(phase)], axis=1) / math.sqrt(NFFT)
    both = both.reshape(NCHAN, 2, 4, 128).transpose(0, 2, 1, 3).reshape(NCHAN, 2 * NFFT)
    high = both.astype(np.float32).astype(ml_dtypes.bfloat16)
    low = (both - high.astype(np.float64)).astype(np.float32).astype(ml_dtypes.bfloat16)
    return high, low


def rows_by(left, right):
    return lax.dot_general(
        left, right, (((1,), (1,)), ((), ())), preferred_element_type=jnp.float32
    )


def times(left, right):
    return jnp.dot(left, right, preferred_element_type=jnp.float32)


def one_hot(found):
    return jnp.where(found, 1.0, 0.0).astype(jnp.bfloat16)


def exchange_kernel(
    volts, taps, owner, assign, table_hi, table_lo, out,
    vbuf, tap_v, tapx, own_v, asg_v, thi, tlo, filt, ghi, glo, wsel, perm, hot_a, hot_b,
    send_a, send_b, recv_a, recv_b, stage_a, stage_b, x_a, x_b, spread, made,
    ready, lsem, osem, za_s, za_r, xb_s, xb_r, zb_s, zb_r, xa_s, xa_r, fa_s, fa_r, fb_s, fb_r,
):
    chan, row, col = lax.axis_index("chan"), lax.axis_index("row"), lax.axis_index("col")
    z, o = chan // 2, chan % 2 * 8 + col

    def device(zz, oo, rr):
        return (zz * 2 + oo // 8, rr, oo % 8)

    def later(base, step):
        return lax.rem(base + step, 16)

    barrier = pltpu.get_barrier_semaphore()

    def greet(d, carry):
        pl.semaphore_signal(barrier, inc=1, device_id=device(later(z, d), o, row), device_id_type=MESH)
        pl.semaphore_signal(barrier, inc=1, device_id=device(later(z, 16 - d), o, row), device_id_type=MESH)
        return carry

    def greet_plane(d, carry):
        pl.semaphore_signal(barrier, inc=1, device_id=device(z, later(o, d), row), device_id_type=MESH)
        return carry

    lax.fori_loop(1, 5, greet, 0)
    lax.fori_loop(1, 16, greet_plane, 0)
    pl.semaphore_signal(barrier, inc=1, device_id=device(z, o, 1 - row), device_id_type=MESH)

    loads = [
        pltpu.make_async_copy(volts.at[:, 0], vbuf.at[0], lsem.at[0]),
        pltpu.make_async_copy(volts.at[:, 1], vbuf.at[1], lsem.at[1]),
        pltpu.make_async_copy(taps, tap_v, lsem.at[2]),
        pltpu.make_async_copy(owner, own_v, lsem.at[3]),
        pltpu.make_async_copy(assign, asg_v, lsem.at[4]),
        pltpu.make_async_copy(table_hi, thi, lsem.at[5]),
        pltpu.make_async_copy(table_lo, tlo, lsem.at[6]),
    ]
    for k in (3, 2, 0, 5, 6, 1, 4):
        loads[k].start()

    def far(i):
        return 8 + (1 - 2 * lax.rem(i, 2)) * ((i + 1) // 2)

    def copy_za(d):
        t = later(z, d)
        return pltpu.make_async_remote_copy(
            send_a.at[t], recv_a.at[z], za_s.at[d], za_r.at[d], device_id=device(t, o, row), device_id_type=MESH)

    def copy_xb(d):
        t = later(o, d)
        return pltpu.make_async_remote_copy(
            send_b.at[t], recv_b.at[o], xb_s.at[d], xb_r.at[d], device_id=device(z, t, row), device_id_type=MESH)

    def copy_zb(d):
        t = later(z, d)
        return pltpu.make_async_remote_copy(
            stage_b.at[t], x_b.at[row * 16 + z], zb_s.at[d], zb_r.at[d], device_id=device(t, o, row), device_id_type=MESH)

    def copy_xa(d):
        t = later(o, d)
        return pltpu.make_async_remote_copy(
            stage_a.at[t], x_a.at[row * 16 + o], xa_s.at[d], xa_r.at[d], device_id=device(z, t, row), device_id_type=MESH)

    def forward_a():
        half = pl.ds(row * 16, 16)
        return pltpu.make_async_remote_copy(
            x_a.at[half], x_a.at[half], fa_s, fa_r, device_id=device(z, o, 1 - row), device_id_type=MESH)

    def forward_b(block):
        return pltpu.make_async_remote_copy(
            x_b.at[row * 16 + block], x_b.at[row * 16 + block], fb_s.at[block], fb_r.at[block],
            device_id=device(z, o, 1 - row), device_id_type=MESH)

    def each(action):
        def step(i, carry):
            action(far(i))
            return carry

        lax.fori_loop(0, 15, step, 0)

    def choose(swapped):
        line = lax.broadcasted_iota(jnp.int32, (256, NCHAN), 0)
        owner_of_line = (line % 16) * 16 + line // 16 if swapped else line
        owned = jnp.where(own_v[...].reshape(1, NCHAN) == owner_of_line, 1.0, 0.0)
        before = jnp.where(
            lax.broadcasted_iota(jnp.int32, (NCHAN, NCHAN), 0)
            < lax.broadcasted_iota(jnp.int32, (NCHAN, NCHAN), 1), 1.0, 0.0).astype(jnp.bfloat16)
        earlier = times(owned.astype(jnp.bfloat16), before)
        for slot in range(2):
            taken = jnp.where(earlier == float(slot), owned, 0.0).astype(jnp.bfloat16)
            wsel[:, slot * 16 : slot * 16 + 16, :] = taken.reshape(16, 16, NCHAN)

    def spectra(pol):
        loads[pol].wait()
        if pol == 0:
            loads[2].wait()
            for m in range(TAPS):
                for j in range(4):
                    line = tap_v[m : m + 1, j * 128 : j * 128 + 128]
                    tapx[m, 2 * j : 2 * j + 2, :] = jnp.broadcast_to(line, (2, 128))
        weights = [tapx[m] for m in range(TAPS)]

        def chunk(i, carry):
            first = i * 8
            for b in range(BATCHES):
                signal = [vbuf[pol, b, first + t].astype(jnp.float32) for t in range(15)]
                for s in range(8):
                    total = weights[0] * signal[s]
                    for m in range(1, TAPS):
                        total = total + weights[m] * signal[s + m]
                    filt[pl.ds(pl.multiple_of((b * SPEC_B + first + s) * 8, 8), 8), :] = total
            return carry

        lax.fori_loop(0, SPEC_B // 8, chunk, 0)
        for q in range(8):
            value = filt[pl.ds(q, SPEC, stride=8), :]
            high = value.astype(jnp.bfloat16)
            low = (value - high.astype(jnp.float32)).astype(jnp.bfloat16)
            here = slice(q * 128, q * 128 + 128)
            other = slice((q ^ 1) * 128, (q ^ 1) * 128 + 128)
            for held, part in ((ghi, high), (glo, low)):
                held[:SPEC, here] = part
                held[SPEC:, other] = part if q % 2 else -part
        if pol == 0:
            loads[5].wait()
            loads[6].wait()
        total = rows_by(thi[...], ghi[...]) + (rows_by(tlo[...], ghi[...]) + rows_by(thi[...], glo[...]))
        return total.astype(jnp.bfloat16)

    def chosen(pol):
        picked = times(wsel[...].reshape(512, NCHAN), spectra(pol))
        return picked.astype(jnp.bfloat16).reshape(16, 32, WIDTH)

    def regroup(ref):
        return times(perm[...], ref[...].reshape(512, WIDTH)).astype(jnp.bfloat16).reshape(16, 32, WIDTH)

    loads[3].wait()
    choose(False)
    send_a[...] = chosen(0)
    pl.semaphore_wait(barrier, 24)
    for d in (4, 12):
        pl.semaphore_signal(ready, inc=1, device_id=device(later(z, d), o, row), device_id_type=MESH)

    def start_near(d, carry):
        copy_za(d).start()
        copy_za(16 - d).start()
        return carry

    def start_far(d, carry):
        copy_za(d).start()
        return carry

    lax.fori_loop(1, 5, start_near, 0)
    recv_a[z] = send_a[z]

    choose(True)
    send_b[...] = chosen(1)
    each(lambda d: copy_xb(d).start())
    pl.semaphore_wait(ready, 2)
    lax.fori_loop(5, 12, start_far, 0)
    recv_b[o] = send_b[o]

    to = lax.broadcasted_iota(jnp.int32, (512, 512), 0)
    perm[...] = one_hot(
        (to % 16) * 32 + (to // 16 % 2) * 16 + to // 32 == lax.broadcasted_iota(jnp.int32, (512, 512), 1))
    loads[4].wait()
    placed = jnp.broadcast_to(asg_v[...], (128, 512)).T
    for t in range(4):
        k = lax.broadcasted_iota(jnp.int32, (512, 128), 1) + t * 128
        r, up, low = k // 256, k // 16 % 16, k % 16
        hot_a[:, t * 128 : t * 128 + 128] = one_hot(placed == low * 32 + up // 8 * 16 + r * 8 + up % 8)
        hot_b[:, t * 128 : t * 128 + 128] = one_hot(placed == up * 32 + low // 8 * 16 + r * 8 + low % 8)

    def ordered(hot, held, pol):
        for slot in range(2):
            lines = held[:, slot * 16 : slot * 16 + 16, :].reshape(512, WIDTH)
            value = times(hot[...], lines)
            for t in range(3):
                spread[slot, t, pl.ds(pol, 512, stride=2), :] = value[:, t * 128 : t * 128 + 128]

    each(lambda d: copy_xb(d).wait_recv())
    stage_b[...] = regroup(recv_b)
    each(lambda d: copy_zb(d).start())
    x_b[row * 16 + z] = stage_b[z]
    forward_b(z).start()

    each(lambda d: copy_za(d).wait_recv())
    stage_a[...] = regroup(recv_a)
    each(lambda d: copy_xa(d).start())
    x_a[row * 16 + o] = stage_a[o]

    each(lambda d: copy_xa(d).wait_recv())
    forward_a().start()

    def pass_on(i, carry):
        d = far(i)
        copy_zb(d).wait_recv()
        forward_b(later(z, 16 - d)).start()
        return carry

    forward_a().wait_recv()
    ordered(hot_a, x_a, 0)
    lax.fori_loop(0, 15, pass_on, 0)

    def arrived(block, carry):
        forward_b(block).wait_recv()
        return carry

    lax.fori_loop(0, 16, arrived, 0)
    ordered(hot_b, x_b, 1)
    stores = [pltpu.make_async_copy(made.at[slot], out.at[slot], osem.at[slot]) for slot in range(2)]
    for slot in range(2):
        for t in range(3):
            made[slot, :, t * 128 : t * 128 + 128] = spread[slot, t].astype(jnp.bfloat16)
        stores[slot].start()

    each(lambda d: copy_za(d).wait_send())
    each(lambda d: copy_xb(d).wait_send())
    each(lambda d: copy_zb(d).wait_send())
    each(lambda d: copy_xa(d).wait_send())
    forward_a().wait_send()

    def left(block, carry):
        forward_b(block).wait_send()
        return carry

    lax.fori_loop(0, 16, left, 0)
    for store in stores:
        store.wait()


def exchange(volts, taps, owner_map, assign):
    high, low = dft_tables()
    held = lambda *shape: pltpu.VMEM(shape, jnp.bfloat16)
    dma = pltpu.SemaphoreType.DMA
    block = (16, 32, WIDTH)
    return pl.pallas_call(
        exchange_kernel,
        out_shape=jax.ShapeDtypeStruct((2, 1024, WIDTH), jnp.bfloat16),
        in_specs=[pl.BlockSpec(memory_space=pl.ANY)] * 6,
        out_specs=pl.BlockSpec(memory_space=pl.ANY),
        scratch_shapes=[
            held(2, BATCHES, BLOCKS, 8, 128),
            pltpu.VMEM((TAPS, NFFT), jnp.float32),
            pltpu.VMEM((TAPS, 8, 128), jnp.float32),
            pltpu.VMEM((NCHAN,), jnp.int32),
            pltpu.VMEM((1, 512), jnp.int32),
            held(NCHAN, 2 * NFFT),
            held(NCHAN, 2 * NFFT),
            pltpu.VMEM((SPEC * 8, 128), jnp.float32),
            held(WIDTH, 2 * NFFT),
            held(WIDTH, 2 * NFFT),
            held(16, 32, NCHAN),
            held(512, 512),
            held(512, 512),
            held(512, 512),
            held(*block),
            held(*block),
            held(*block),
            held(*block),
            held(*block),
            held(*block),
            held(32, 32, WIDTH),
            held(32, 32, WIDTH),
            pltpu.VMEM((2, 3, 1024, 128), jnp.float32),
            held(2, 1024, WIDTH),
            pltpu.SemaphoreType.REGULAR,
            dma((7,)), dma((2,)),
            dma((16,)), dma((16,)), dma((16,)), dma((16,)), dma((16,)), dma((16,)), dma((16,)), dma((16,)),
            dma, dma, dma((16,)), dma((16,)),
        ],
        compiler_params=pltpu.CompilerParams(
            collective_id=0, has_side_effects=True, vmem_limit_bytes=60 << 20
        ),
        name="exchange",
    )(volts, taps, owner_map, assign, jnp.asarray(high), jnp.asarray(low))


def visibility_kernel(lines, out, held, turned, made, lsem, osem):
    loads = [pltpu.make_async_copy(lines.at[slot], held.at[slot], lsem.at[slot]) for slot in range(2)]
    for load in loads:
        load.start()
    half = pl.multiple_of(lax.axis_index("row") * 512, 512)
    first = lax.broadcasted_iota(jnp.int32, (512, WIDTH), 1) < SPEC
    scale = 1.0 / math.sqrt(WIDTH)
    stores = []
    for slot in range(2):
        loads[slot].wait()
        rolled = pltpu.roll(held[slot, pl.ds(half, 512), :].astype(jnp.float32), SPEC, 1)
        turned[...] = jnp.where(first, rolled, -rolled).astype(jnp.bfloat16)
        for part in range(2):
            ours = turned[...] if part else held[slot, pl.ds(half, 512), :]
            made[slot, part] = (rows_by(ours, held[slot]) * scale).astype(jnp.bfloat16)
            stores.append(pltpu.make_async_copy(made.at[slot, part], out.at[slot, part], osem.at[2 * slot + part]))
            stores[-1].start()
    for store in stores:
        store.wait()


def visibilities(lines):
    return pl.pallas_call(
        visibility_kernel,
        out_shape=jax.ShapeDtypeStruct((2, 2, 512, 1024), jnp.bfloat16),
        in_specs=[pl.BlockSpec(memory_space=pl.ANY)],
        out_specs=pl.BlockSpec(memory_space=pl.ANY),
        scratch_shapes=[
            pltpu.VMEM((2, 1024, WIDTH), jnp.bfloat16),
            pltpu.VMEM((512, WIDTH), jnp.bfloat16),
            pltpu.VMEM((2, 2, 512, 1024), jnp.bfloat16),
            pltpu.SemaphoreType.DMA((2,)),
            pltpu.SemaphoreType.DMA((4,)),
        ],
        compiler_params=pltpu.CompilerParams(vmem_limit_bytes=60 << 20),
        name="visibilities",
    )(lines)


def shards(volts, taps, owner_map, assign):
    blocks = volts.reshape(BATCHES, 2, 2, BLOCKS, 4, 128).transpose(0, 1, 3, 4, 2, 5)
    lines = exchange(
        blocks.reshape(BATCHES, 2, BLOCKS, 8, 128),
        taps,
        owner_map,
        assign.reshape(1, 512),
    )
    return visibilities(lines)


def solution(mesh):
    placed = (P(None, ("chan", "row", "col"), None, None), P(), P(), P())
    return jax.shard_map(
        shards,
        mesh=mesh,
        in_specs=placed,
        out_specs=P(("chan", "col"), None, "row", None),
        check_vma=False,
    )
```

```python
import functools
import math

import jax
import jax.numpy as jnp
import ml_dtypes
import numpy as np
from jax import lax
from jax.experimental import pallas as pl
from jax.experimental.pallas import tpu as pltpu
from jax.sharding import PartitionSpec as P

NFFT = 512
TAPS = 8
BATCHES = 2
SPEC_B = 96
NCHAN = 384
BLOCKS = SPEC_B + TAPS - 1
SPEC = BATCHES * SPEC_B
WIDTH = 2 * SPEC
MESH = pl.DeviceIdType.MESH


CLASSES = 4
PER_CLASS = NCHAN // CLASSES


def dft_tables():
    channel = np.arange(PER_CLASS)[None, :, None] * CLASSES + np.arange(CLASSES)[:, None, None]
    phase = 2.0 * np.pi / NFFT * (channel * np.arange(128) % NFFT)
    both = np.concatenate([np.cos(phase), np.sin(phase)], axis=2) / math.sqrt(NFFT)
    high = both.astype(np.float32).astype(ml_dtypes.bfloat16)
    low = (both - high.astype(np.float64)).astype(np.float32).astype(ml_dtypes.bfloat16)
    return np.concatenate([high, low], axis=1)


def rows_by(left, right):
    return lax.dot_general(
        left, right, (((1,), (1,)), ((), ())), preferred_element_type=jnp.float32
    )


def times(left, right):
    return jnp.dot(left, right, preferred_element_type=jnp.float32)


def one_hot(found):
    return jnp.where(found, 1.0, 0.0).astype(jnp.bfloat16)


def exchange_kernel(
    volts, taps, owner, assign, table, out,
    vbuf, tap_v, tapx, own_v, asg_v, tab_v, owners, before, filt, ghi, glo, spec, wsel, perm, hot_a, hot_b,
    send_a, send_b, recv_a, recv_b, stage_a, stage_b, x_a, x_b, partial, spread, made,
    ready, lsem, osem, za_s, za_r, xb_s, xb_r, zb_s, zb_r, xa_s, xa_r, fa_s, fa_r, fb_s, fb_r,
):
    chan, row, col = lax.axis_index("chan"), lax.axis_index("row"), lax.axis_index("col")
    z, o = chan // 2, chan % 2 * 8 + col

    def device(zz, oo, rr):
        return (zz * 2 + oo // 8, rr, oo % 8)

    def later(base, step):
        return lax.rem(base + step, 16)

    loads = [
        pltpu.make_async_copy(volts.at[:, 0], vbuf.at[0], lsem.at[0]),
        pltpu.make_async_copy(volts.at[:, 1], vbuf.at[1], lsem.at[1]),
        pltpu.make_async_copy(taps, tap_v, lsem.at[2]),
        pltpu.make_async_copy(owner, own_v, lsem.at[3]),
        pltpu.make_async_copy(assign, asg_v, lsem.at[4]),
        pltpu.make_async_copy(table, tab_v, lsem.at[5]),
    ]
    for k in (3, 0, 2, 5, 1, 4):
        loads[k].start()

    barrier = pltpu.get_barrier_semaphore()

    def greet(d, carry):
        pl.semaphore_signal(barrier, inc=1, device_id=device(later(z, d), o, row), device_id_type=MESH)
        pl.semaphore_signal(barrier, inc=1, device_id=device(later(z, 16 - d), o, row), device_id_type=MESH)
        return carry

    def greet_plane(d, carry):
        pl.semaphore_signal(barrier, inc=1, device_id=device(z, later(o, d), row), device_id_type=MESH)
        return carry

    lax.fori_loop(1, 5, greet, 0)
    lax.fori_loop(1, 16, greet_plane, 0)
    pl.semaphore_signal(barrier, inc=1, device_id=device(z, o, 1 - row), device_id_type=MESH)

    def far(i):
        return 8 + (1 - 2 * lax.rem(i, 2)) * ((i + 1) // 2)

    def copy_za(d):
        t = later(z, d)
        return pltpu.make_async_remote_copy(
            send_a.at[t], recv_a.at[z], za_s.at[d], za_r.at[d], device_id=device(t, o, row), device_id_type=MESH)

    def copy_xb(d):
        t = later(o, d)
        return pltpu.make_async_remote_copy(
            send_b.at[t], recv_b.at[o], xb_s.at[d], xb_r.at[d], device_id=device(z, t, row), device_id_type=MESH)

    def copy_zb(d):
        t = later(z, d)
        return pltpu.make_async_remote_copy(
            stage_b.at[t], x_b.at[z], zb_s.at[d], zb_r.at[d], device_id=device(t, o, row), device_id_type=MESH)

    def copy_xa(d):
        t = later(o, d)
        return pltpu.make_async_remote_copy(
            stage_a.at[t], x_a.at[o], xa_s.at[d], xa_r.at[d], device_id=device(z, t, row), device_id_type=MESH)

    def forward_a():
        return pltpu.make_async_remote_copy(
            x_a.at[pl.ds(0, 16)], x_a.at[pl.ds(16, 16)], fa_s, fa_r, device_id=device(z, o, 1 - row), device_id_type=MESH)

    def forward_b(block):
        return pltpu.make_async_remote_copy(
            x_b.at[block], x_b.at[16 + block], fb_s, fb_r,
            device_id=device(z, o, 1 - row), device_id_type=MESH)

    def each(action):
        def step(i, carry):
            action(far(i))
            return carry

        lax.fori_loop(0, 15, step, 0)

    def choose(swapped):
        line = lax.broadcasted_iota(jnp.int32, (256, NCHAN), 0)
        owner_of_line = (line % 16) * 16 + line // 16 if swapped else line
        owned = jnp.where(owners[0:1, :] == owner_of_line.astype(jnp.float32), 1.0, 0.0)
        earlier = times(owned.astype(jnp.bfloat16), before[...])
        for slot in range(2):
            taken = jnp.where(earlier == float(slot), owned, 0.0).astype(jnp.bfloat16)
            wsel[:, slot * 16 : slot * 16 + 16, :] = taken.reshape(16, 16, NCHAN)

    def spectra(pol):
        loads[pol].wait()
        if pol == 0:
            loads[2].wait()
            for m in range(TAPS):
                for j in range(4):
                    line = tap_v[m : m + 1, j * 128 : j * 128 + 128]
                    tapx[m, 2 * j : 2 * j + 2, :] = jnp.broadcast_to(line, (2, 128))
        weights = [tapx[m] for m in range(TAPS)]

        def chunk(i, carry):
            first = i * 8
            for b in range(BATCHES):
                signal = [vbuf[pol, b, first + t].astype(jnp.float32) for t in range(15)]
                for s in range(8):
                    total = weights[0] * signal[s]
                    for m in range(1, TAPS):
                        total = total + weights[m] * signal[s + m]
                    filt[pl.ds(pl.multiple_of((b * SPEC_B + first + s) * 8, 8), 8), :] = total
            return carry

        lax.fori_loop(0, SPEC_B // 8, chunk, 0)
        for top in range(0, SPEC, 32):
            x = [filt[pl.ds(8 * top + q, 32, stride=8), :] for q in range(8)]
            (er, ei), (dr, di) = ((x[0] + x[4], x[1] + x[5]), (x[0] - x[4], x[1] - x[5]))
            (fr, fi), (gr, gi) = ((x[2] + x[6], x[3] + x[7]), (x[2] - x[6], x[3] - x[7]))
            folded = ((er + fr, ei + fi), (dr + gi, di - gr), (er - fr, ei - fi), (dr - gi, di + gr))
            for r in range(CLASSES):
                for a in range(2):
                    value = folded[r][a]
                    high = value.astype(jnp.bfloat16)
                    low = (value - high.astype(jnp.float32)).astype(jnp.bfloat16)
                    here, other = slice(a * 128, a * 128 + 128), slice(128 - a * 128, 256 - a * 128)
                    for held, part in ((ghi, high), (glo, low)):
                        held[r, top : top + 32, here] = part
                        held[r, SPEC + top : SPEC + top + 32, other] = part if a else -part
        if pol == 0:
            loads[5].wait()
        for r in range(CLASSES):
            both = rows_by(tab_v[r], ghi[r])
            small = rows_by(tab_v[r, :PER_CLASS], glo[r])
            total = both[:PER_CLASS] + (both[PER_CLASS:] + small)
            spec[r * PER_CLASS : r * PER_CLASS + PER_CLASS, :] = total.astype(jnp.bfloat16)

    def chosen(pol):
        spectra(pol)
        picked = times(wsel[...].reshape(512, NCHAN), spec[...])
        return picked.astype(jnp.bfloat16).reshape(16, 32, WIDTH)

    def regroup(ref):
        return times(perm[...], ref[...].reshape(512, WIDTH)).astype(jnp.bfloat16).reshape(16, 32, WIDTH)

    loads[3].wait()
    def channel_at(axis):
        i = lax.broadcasted_iota(jnp.int32, (NCHAN, NCHAN), axis)
        steps = [jnp.where(i >= r * PER_CLASS, 1, 0) for r in range(1, CLASSES)]
        return 4 * i - (NCHAN - 1) * (steps[0] + steps[1] + steps[2])

    moved = one_hot(lax.broadcasted_iota(jnp.int32, (NCHAN, NCHAN), 0) == channel_at(1))
    line = jnp.broadcast_to(own_v[...].reshape(1, NCHAN), (8, NCHAN))
    owners[...] = times(line.astype(jnp.float32).astype(jnp.bfloat16), moved)
    before[...] = one_hot(channel_at(0) < channel_at(1))
    choose(False)
    send_a[...] = chosen(0)
    pl.semaphore_wait(barrier, 24)
    for d in (4, 12):
        pl.semaphore_signal(ready, inc=1, device_id=device(later(z, d), o, row), device_id_type=MESH)

    def start_near(d, carry):
        copy_za(d).start()
        copy_za(16 - d).start()
        return carry

    def start_far(i, carry):
        copy_za(far(i)).start()
        return carry

    lax.fori_loop(1, 5, start_near, 0)
    recv_a[z] = send_a[z]

    choose(True)
    send_b[...] = chosen(1)
    each(lambda d: copy_xb(d).start())
    pl.semaphore_wait(ready, 2)
    lax.fori_loop(0, 7, start_far, 0)
    recv_b[o] = send_b[o]

    to = lax.broadcasted_iota(jnp.int32, (512, 512), 0)
    perm[...] = one_hot(
        (to % 16) * 32 + (to // 16 % 2) * 16 + to // 32 == lax.broadcasted_iota(jnp.int32, (512, 512), 1))
    loads[4].wait()
    placed = jnp.broadcast_to(asg_v[...], (128, 512)).T
    for t in range(4):
        k = lax.broadcasted_iota(jnp.int32, (512, 128), 1) + t * 128
        r, up, low = row if t < 2 else 1 - row, k // 16 % 16, k % 16
        hot_a[:, t * 128 : t * 128 + 128] = one_hot(placed == low * 32 + up // 8 * 16 + r * 8 + up % 8)
        hot_b[:, t * 128 : t * 128 + 128] = one_hot(placed == up * 32 + low // 8 * 16 + r * 8 + low % 8)

    def lines_of(held, slot, first, last):
        return held[first:last, slot * 16 : slot * 16 + 16, :].reshape((last - first) * 16, WIDTH)

    def ordered(pol, slot):
        if pol:
            value = partial[slot] + times(hot_b[:, 256:], lines_of(x_b, slot, 16, 32))
        else:
            value = times(hot_a[...], lines_of(x_a, slot, 0, 32))
        for t in range(3):
            spread[slot, t, pl.ds(pol, 512, stride=2), :] = value[:, t * 128 : t * 128 + 128]

    each(lambda d: copy_xb(d).wait_recv())
    stage_b[...] = regroup(recv_b)
    each(lambda d: copy_za(d).wait_send())
    def start_zb(group):
        def step(i, carry):
            t = group * 8 + lax.rem(z + 4 + i, 8)

            @pl.when(t != z)
            def _():
                copy_zb(later(t, 16 - z)).start()

            return carry

        lax.fori_loop(0, 8, step, 0)

    for group in (0,):
        start_zb(group)
    x_b[z] = stage_b[z]
    forward_b(z).start()

    each(lambda d: copy_za(d).wait_recv())
    stage_a[...] = regroup(recv_a)
    each(lambda d: copy_xa(d).start())
    for group in (1,):
        start_zb(group)
    x_a[o] = stage_a[o]

    each(lambda d: copy_xb(d).wait_send())
    each(lambda d: copy_xa(d).wait_recv())
    forward_a().start()
    each(lambda d: copy_xa(d).wait_send())

    def pass_on(i, carry):
        d = far(i)
        copy_zb(d).wait()
        forward_b(later(z, 16 - d)).start()
        return carry

    forward_a().wait()
    for slot in range(2):
        ordered(0, slot)
    lax.fori_loop(0, 15, pass_on, 0)
    for slot in range(2):
        partial[slot] = times(hot_b[:, :256], lines_of(x_b, slot, 0, 16))

    pltpu.make_async_copy(x_b.at[pl.ds(16, 16)], x_b.at[pl.ds(16, 16)], fb_r).wait()
    stores = [pltpu.make_async_copy(made.at[slot], out.at[slot], osem.at[slot]) for slot in range(2)]
    for slot in range(2):
        ordered(1, slot)
        for t in range(3):
            made[slot, :, t * 128 : t * 128 + 128] = spread[slot, t].astype(jnp.bfloat16)
        stores[slot].start()
    pltpu.make_async_copy(x_b.at[pl.ds(0, 16)], x_b.at[pl.ds(0, 16)], fb_s).wait()
    for store in stores:
        store.wait()


def exchange(volts, taps, owner_map, assign):
    held = lambda *shape: pltpu.VMEM(shape, jnp.bfloat16)
    dma = pltpu.SemaphoreType.DMA
    block = (16, 32, WIDTH)
    return pl.pallas_call(
        exchange_kernel,
        out_shape=jax.ShapeDtypeStruct((2, 1024, WIDTH), jnp.bfloat16),
        in_specs=[pl.BlockSpec(memory_space=pl.ANY)] * 5,
        out_specs=pl.BlockSpec(memory_space=pl.ANY),
        scratch_shapes=[
            held(2, BATCHES, BLOCKS, 8, 128),
            pltpu.VMEM((TAPS, NFFT), jnp.float32),
            pltpu.VMEM((TAPS, 8, 128), jnp.float32),
            pltpu.VMEM((NCHAN,), jnp.int32),
            pltpu.VMEM((1, 512), jnp.int32),
            held(CLASSES, 2 * PER_CLASS, 256),
            pltpu.VMEM((8, NCHAN), jnp.float32),
            held(NCHAN, NCHAN),
            pltpu.VMEM((SPEC * 8, 128), jnp.float32),
            held(CLASSES, WIDTH, 256),
            held(CLASSES, WIDTH, 256),
            held(NCHAN, WIDTH),
            held(16, 32, NCHAN),
            held(512, 512),
            held(512, 512),
            held(512, 512),
            held(*block),
            held(*block),
            held(*block),
            held(*block),
            held(*block),
            held(*block),
            held(32, 32, WIDTH),
            held(32, 32, WIDTH),
            pltpu.VMEM((2, 512, WIDTH), jnp.float32),
            pltpu.VMEM((2, 3, 1024, 128), jnp.float32),
            held(2, 1024, WIDTH),
            pltpu.SemaphoreType.REGULAR,
            dma((6,)), dma((2,)),
            dma((16,)), dma((16,)), dma((16,)), dma((16,)), dma((16,)), dma((16,)), dma((16,)), dma((16,)),
            dma, dma, dma, dma,
        ],
        compiler_params=pltpu.CompilerParams(
            collective_id=0, has_side_effects=True, vmem_limit_bytes=60 << 20
        ),
        name="exchange",
    )(volts, taps, owner_map, assign, jnp.asarray(dft_tables()))


def visibility_kernel(lines, out, held, turned, made, lsem, osem):
    half = lax.axis_index("row") * 512
    loads = [pltpu.make_async_copy(lines.at[slot], held.at[slot], lsem.at[slot]) for slot in range(2)]
    for load in loads:
        load.start()
    first = lax.broadcasted_iota(jnp.int32, (512, WIDTH), 1) < SPEC
    scale = 1.0 / math.sqrt(WIDTH)
    stores = []
    for slot in range(2):
        loads[slot].wait()
        ours = held[slot, pl.ds(pl.multiple_of(half, 512), 512), :].astype(jnp.float32)
        rolled = pltpu.roll(ours, SPEC, 1)
        turned[slot] = jnp.where(first, rolled, -rolled).astype(jnp.bfloat16)
        for part in range(2):
            for top in (0, 256):
                rows = pl.ds(top, 256)
                left = turned[slot, rows] if part else held[slot, pl.ds(pl.multiple_of(half + top, 256), 256), :]
                made[slot, part, rows] = (rows_by(left, held[slot]) * scale).astype(jnp.bfloat16)
                stores.append(
                    pltpu.make_async_copy(made.at[slot, part, rows], out.at[slot, part, rows], osem.at[len(stores)]))
                stores[-1].start()
    for store in stores:
        store.wait()


def visibilities(lines):
    return pl.pallas_call(
        visibility_kernel,
        out_shape=jax.ShapeDtypeStruct((2, 2, 512, 1024), jnp.bfloat16),
        in_specs=[pl.BlockSpec(memory_space=pl.ANY)],
        out_specs=pl.BlockSpec(memory_space=pl.ANY),
        scratch_shapes=[
            pltpu.VMEM((2, 1024, WIDTH), jnp.bfloat16),
            pltpu.VMEM((2, 512, WIDTH), jnp.bfloat16),
            pltpu.VMEM((2, 2, 512, 1024), jnp.bfloat16),
            pltpu.SemaphoreType.DMA((2,)),
            pltpu.SemaphoreType.DMA((8,)),
        ],
        compiler_params=pltpu.CompilerParams(vmem_limit_bytes=60 << 20),
        name="visibilities",
    )(lines)


def shards(volts, taps, owner_map, assign):
    blocks = volts.reshape(BATCHES, 2, 2, BLOCKS, 4, 128).transpose(0, 1, 3, 4, 2, 5)
    lines = exchange(
        blocks.reshape(BATCHES, 2, BLOCKS, 8, 128),
        taps,
        owner_map,
        assign.reshape(1, 512),
    )
    return visibilities(lines)


def solution(mesh):
    placed = (P(None, ("chan", "row", "col"), None, None), P(), P(), P())
    return jax.shard_map(
        shards,
        mesh=mesh,
        in_specs=placed,
        out_specs=P(("chan", "col"), None, "row", None),
        check_vma=False,
    )
```

```python
import functools
import math

import jax
import jax.numpy as jnp
import ml_dtypes
import numpy as np
from jax import lax
from jax.experimental import pallas as pl
from jax.experimental.pallas import tpu as pltpu
from jax.sharding import PartitionSpec as P

NFFT = 512
TAPS = 8
BATCHES = 2
SPEC_B = 96
NCHAN = 384
BLOCKS = SPEC_B + TAPS - 1
SPEC = BATCHES * SPEC_B
WIDTH = 2 * SPEC
MESH = pl.DeviceIdType.MESH


CLASSES = 4
PER_CLASS = NCHAN // CLASSES


def dft_tables():
    channel = np.arange(PER_CLASS)[None, :, None] * CLASSES + np.arange(CLASSES)[:, None, None]
    phase = 2.0 * np.pi / NFFT * (channel * np.arange(128) % NFFT)
    both = np.concatenate([np.cos(phase), np.sin(phase)], axis=2) / math.sqrt(NFFT)
    high = both.astype(np.float32).astype(ml_dtypes.bfloat16)
    low = (both - high.astype(np.float64)).astype(np.float32).astype(ml_dtypes.bfloat16)
    return np.concatenate([high, low], axis=1)


def rows_by(left, right):
    return lax.dot_general(
        left, right, (((1,), (1,)), ((), ())), preferred_element_type=jnp.float32
    )


def times(left, right):
    return jnp.dot(left, right, preferred_element_type=jnp.float32)


def one_hot(found):
    return jnp.where(found, 1.0, 0.0).astype(jnp.bfloat16)


def exchange_kernel(
    volts, taps, owner, assign, table, out,
    vbuf, tap_v, tapx, own_v, asg_v, tab_v, owners, before, filt, ghi, glo, spec, wsel, perm, hot_a, hot_b,
    send_a, send_b, recv_a, recv_b, stage_a, stage_b, x_a, x_b, partial, spread, made,
    ready, lsem, osem, za_s, za_r, xb_s, xb_r, zb_s, zb_r, xa_s, xa_r, fa_s, fa_r, fb_s, fb_r,
):
    chan, row, col = lax.axis_index("chan"), lax.axis_index("row"), lax.axis_index("col")
    z, o = chan // 2, chan % 2 * 8 + col

    def device(zz, oo, rr):
        return (zz * 2 + oo // 8, rr, oo % 8)

    def later(base, step):
        return lax.rem(base + step, 16)

    loads = [
        pltpu.make_async_copy(volts.at[:, 0], vbuf.at[0], lsem.at[0]),
        pltpu.make_async_copy(volts.at[:, 1], vbuf.at[1], lsem.at[1]),
        pltpu.make_async_copy(taps, tap_v, lsem.at[2]),
        pltpu.make_async_copy(owner, own_v, lsem.at[3]),
        pltpu.make_async_copy(assign, asg_v, lsem.at[4]),
        pltpu.make_async_copy(table, tab_v, lsem.at[5]),
    ]
    for k in (3, 0, 2, 5, 1, 4):
        loads[k].start()

    barrier = pltpu.get_barrier_semaphore()

    def greet(d, carry):
        pl.semaphore_signal(barrier, inc=1, device_id=device(later(z, d), o, row), device_id_type=MESH)
        pl.semaphore_signal(barrier, inc=1, device_id=device(later(z, 16 - d), o, row), device_id_type=MESH)
        return carry

    def greet_plane(d, carry):
        pl.semaphore_signal(barrier, inc=1, device_id=device(z, later(o, d), row), device_id_type=MESH)
        return carry

    lax.fori_loop(1, 5, greet, 0)
    lax.fori_loop(1, 16, greet_plane, 0)
    pl.semaphore_signal(barrier, inc=1, device_id=device(z, o, 1 - row), device_id_type=MESH)

    def far(i):
        return 8 + (1 - 2 * lax.rem(i, 2)) * ((i + 1) // 2)

    def copy_za(d):
        t = later(z, d)
        return pltpu.make_async_remote_copy(
            send_a.at[t], recv_a.at[z], za_s.at[d], za_r.at[d], device_id=device(t, o, row), device_id_type=MESH)

    def copy_xb(d):
        t = later(o, d)
        return pltpu.make_async_remote_copy(
            send_b.at[t], recv_b.at[o], xb_s.at[d], xb_r.at[d], device_id=device(z, t, row), device_id_type=MESH)

    def copy_zb(d):
        t = later(z, d)
        return pltpu.make_async_remote_copy(
            stage_b.at[t], x_b.at[z], zb_s.at[d], zb_r.at[d], device_id=device(t, o, row), device_id_type=MESH)

    def copy_xa(d):
        t = later(o, d)
        return pltpu.make_async_remote_copy(
            stage_a.at[t], x_a.at[o], xa_s.at[d], xa_r.at[d], device_id=device(z, t, row), device_id_type=MESH)

    def forward_a():
        return pltpu.make_async_remote_copy(
            x_a.at[pl.ds(0, 16)], x_a.at[pl.ds(16, 16)], fa_s, fa_r, device_id=device(z, o, 1 - row), device_id_type=MESH)

    def forward_b(block):
        return pltpu.make_async_remote_copy(
            x_b.at[block], x_b.at[16 + block], fb_s, fb_r,
            device_id=device(z, o, 1 - row), device_id_type=MESH)

    def each(action):
        def step(i, carry):
            action(far(i))
            return carry

        lax.fori_loop(0, 15, step, 0)

    def choose(swapped):
        line = lax.broadcasted_iota(jnp.int32, (256, NCHAN), 0)
        owner_of_line = (line % 16) * 16 + line // 16 if swapped else line
        owned = jnp.where(owners[0:1, :] == owner_of_line.astype(jnp.float32), 1.0, 0.0)
        earlier = times(owned.astype(jnp.bfloat16), before[...])
        for slot in range(2):
            taken = jnp.where(earlier == float(slot), owned, 0.0).astype(jnp.bfloat16)
            wsel[:, slot * 16 : slot * 16 + 16, :] = taken.reshape(16, 16, NCHAN)

    def spectra(pol):
        loads[pol].wait()
        if pol == 0:
            loads[2].wait()
            for m in range(TAPS):
                for j in range(4):
                    line = tap_v[m : m + 1, j * 128 : j * 128 + 128]
                    tapx[m, 2 * j : 2 * j + 2, :] = jnp.broadcast_to(line, (2, 128))
        weights = [tapx[m] for m in range(TAPS)]

        def chunk(i, carry):
            first = i * 8
            for b in range(BATCHES):
                signal = [vbuf[pol, b, first + t].astype(jnp.float32) for t in range(15)]
                for s in range(8):
                    total = weights[0] * signal[s]
                    for m in range(1, TAPS):
                        total = total + weights[m] * signal[s + m]
                    filt[pl.ds(pl.multiple_of((b * SPEC_B + first + s) * 8, 8), 8), :] = total
            return carry

        lax.fori_loop(0, SPEC_B // 8, chunk, 0)
        for top in range(0, SPEC, 32):
            x = [filt[pl.ds(8 * top + q, 32, stride=8), :] for q in range(8)]
            (er, ei), (dr, di) = ((x[0] + x[4], x[1] + x[5]), (x[0] - x[4], x[1] - x[5]))
            (fr, fi), (gr, gi) = ((x[2] + x[6], x[3] + x[7]), (x[2] - x[6], x[3] - x[7]))
            folded = ((er + fr, ei + fi), (dr + gi, di - gr), (er - fr, ei - fi), (dr - gi, di + gr))
            for r in range(CLASSES):
                for a in range(2):
                    value = folded[r][a]
                    high = value.astype(jnp.bfloat16)
                    low = (value - high.astype(jnp.float32)).astype(jnp.bfloat16)
                    here, other = slice(a * 128, a * 128 + 128), slice(128 - a * 128, 256 - a * 128)
                    for held, part in ((ghi, high), (glo, low)):
                        held[r, top : top + 32, here] = part
                        held[r, SPEC + top : SPEC + top + 32, other] = part if a else -part
        if pol == 0:
            loads[5].wait()
        for r in range(CLASSES):
            both = rows_by(tab_v[r], ghi[r])
            small = rows_by(tab_v[r, :PER_CLASS], glo[r])
            total = both[:PER_CLASS] + (both[PER_CLASS:] + small)
            spec[r * PER_CLASS : r * PER_CLASS + PER_CLASS, :] = total.astype(jnp.bfloat16)

    def chosen(pol):
        spectra(pol)
        picked = times(wsel[...].reshape(512, NCHAN), spec[...])
        return picked.astype(jnp.bfloat16).reshape(16, 32, WIDTH)

    def regroup(ref):
        return times(perm[...], ref[...].reshape(512, WIDTH)).astype(jnp.bfloat16).reshape(16, 32, WIDTH)

    loads[3].wait()
    def channel_at(axis):
        i = lax.broadcasted_iota(jnp.int32, (NCHAN, NCHAN), axis)
        steps = [jnp.where(i >= r * PER_CLASS, 1, 0) for r in range(1, CLASSES)]
        return 4 * i - (NCHAN - 1) * (steps[0] + steps[1] + steps[2])

    moved = one_hot(lax.broadcasted_iota(jnp.int32, (NCHAN, NCHAN), 0) == channel_at(1))
    line = jnp.broadcast_to(own_v[...].reshape(1, NCHAN), (8, NCHAN))
    owners[...] = times(line.astype(jnp.float32).astype(jnp.bfloat16), moved)
    before[...] = one_hot(channel_at(0) < channel_at(1))
    choose(False)
    send_a[...] = chosen(0)
    pl.semaphore_wait(barrier, 24)
    for d in (4, 12):
        pl.semaphore_signal(ready, inc=1, device_id=device(later(z, d), o, row), device_id_type=MESH)

    def start_near(d, carry):
        copy_za(d).start()
        copy_za(16 - d).start()
        return carry

    def start_far(i, carry):
        copy_za(far(i)).start()
        return carry

    lax.fori_loop(1, 5, start_near, 0)
    recv_a[z] = send_a[z]

    choose(True)
    send_b[...] = chosen(1)
    each(lambda d: copy_xb(d).start())
    pl.semaphore_wait(ready, 2)
    lax.fori_loop(0, 7, start_far, 0)
    recv_b[o] = send_b[o]

    to = lax.broadcasted_iota(jnp.int32, (512, 512), 0)
    perm[...] = one_hot(
        (to % 16) * 32 + (to // 16 % 2) * 16 + to // 32 == lax.broadcasted_iota(jnp.int32, (512, 512), 1))
    loads[4].wait()
    placed = jnp.broadcast_to(asg_v[...], (128, 512)).T
    for t in range(4):
        k = lax.broadcasted_iota(jnp.int32, (512, 128), 1) + t * 128
        r, up, low = row if t < 2 else 1 - row, k // 16 % 16, k % 16
        hot_a[:, t * 128 : t * 128 + 128] = one_hot(placed == low * 32 + up // 8 * 16 + r * 8 + up % 8)
        hot_b[:, t * 128 : t * 128 + 128] = one_hot(placed == up * 32 + low // 8 * 16 + r * 8 + low % 8)

    def lines_of(held, slot, first, last):
        return held[first:last, slot * 16 : slot * 16 + 16, :].reshape((last - first) * 16, WIDTH)

    def ordered(pol, slot):
        if pol:
            value = partial[slot] + times(hot_b[:, 256:], lines_of(x_b, slot, 16, 32))
        else:
            value = times(hot_a[...], lines_of(x_a, slot, 0, 32))
        for t in range(3):
            spread[slot, t, pl.ds(pol, 512, stride=2), :] = value[:, t * 128 : t * 128 + 128]

    each(lambda d: copy_xb(d).wait_recv())
    stage_b[...] = regroup(recv_b)
    each(lambda d: copy_za(d).wait_send())
    def start_zb(i, carry):
        copy_zb(far(i)).start()
        return carry

    lax.fori_loop(0, 7, start_zb, 0)
    x_b[z] = stage_b[z]
    forward_b(z).start()

    each(lambda d: copy_za(d).wait_recv())
    stage_a[...] = regroup(recv_a)
    each(lambda d: copy_xa(d).start())
    lax.fori_loop(7, 15, start_zb, 0)
    x_a[o] = stage_a[o]

    each(lambda d: copy_xb(d).wait_send())
    each(lambda d: copy_xa(d).wait_recv())
    forward_a().start()
    each(lambda d: copy_xa(d).wait_send())

    def pass_on(i, carry):
        d = far(i)
        copy_zb(d).wait()
        forward_b(later(z, 16 - d)).start()
        return carry

    forward_a().wait()
    for slot in range(2):
        ordered(0, slot)
    lax.fori_loop(0, 15, pass_on, 0)
    for slot in range(2):
        partial[slot] = times(hot_b[:, :256], lines_of(x_b, slot, 0, 16))

    pltpu.make_async_copy(x_b.at[pl.ds(16, 16)], x_b.at[pl.ds(16, 16)], fb_r).wait()
    stores = [pltpu.make_async_copy(made.at[slot], out.at[slot], osem.at[slot]) for slot in range(2)]
    for slot in range(2):
        ordered(1, slot)
        for t in range(3):
            made[slot, :, t * 128 : t * 128 + 128] = spread[slot, t].astype(jnp.bfloat16)
        stores[slot].start()
    pltpu.make_async_copy(x_b.at[pl.ds(0, 16)], x_b.at[pl.ds(0, 16)], fb_s).wait()
    for store in stores:
        store.wait()


def exchange(volts, taps, owner_map, assign):
    held = lambda *shape: pltpu.VMEM(shape, jnp.bfloat16)
    dma = pltpu.SemaphoreType.DMA
    block = (16, 32, WIDTH)
    return pl.pallas_call(
        exchange_kernel,
        out_shape=jax.ShapeDtypeStruct((2, 1024, WIDTH), jnp.bfloat16),
        in_specs=[pl.BlockSpec(memory_space=pl.ANY)] * 5,
        out_specs=pl.BlockSpec(memory_space=pl.ANY),
        scratch_shapes=[
            held(2, BATCHES, BLOCKS, 8, 128),
            pltpu.VMEM((TAPS, NFFT), jnp.float32),
            pltpu.VMEM((TAPS, 8, 128), jnp.float32),
            pltpu.VMEM((NCHAN,), jnp.int32),
            pltpu.VMEM((1, 512), jnp.int32),
            held(CLASSES, 2 * PER_CLASS, 256),
            pltpu.VMEM((8, NCHAN), jnp.float32),
            held(NCHAN, NCHAN),
            pltpu.VMEM((SPEC * 8, 128), jnp.float32),
            held(CLASSES, WIDTH, 256),
            held(CLASSES, WIDTH, 256),
            held(NCHAN, WIDTH),
            held(16, 32, NCHAN),
            held(512, 512),
            held(512, 512),
            held(512, 512),
            held(*block),
            held(*block),
            held(*block),
            held(*block),
            held(*block),
            held(*block),
            held(32, 32, WIDTH),
            held(32, 32, WIDTH),
            pltpu.VMEM((2, 512, WIDTH), jnp.float32),
            pltpu.VMEM((2, 3, 1024, 128), jnp.float32),
            held(2, 1024, WIDTH),
            pltpu.SemaphoreType.REGULAR,
            dma((6,)), dma((2,)),
            dma((16,)), dma((16,)), dma((16,)), dma((16,)), dma((16,)), dma((16,)), dma((16,)), dma((16,)),
            dma, dma, dma, dma,
        ],
        compiler_params=pltpu.CompilerParams(
            collective_id=0, has_side_effects=True, vmem_limit_bytes=60 << 20
        ),
        name="exchange",
    )(volts, taps, owner_map, assign, jnp.asarray(dft_tables()))


def visibility_kernel(lines, out, held, turned, made, lsem, osem):
    half = lax.axis_index("row") * 512
    loads = [pltpu.make_async_copy(lines.at[slot], held.at[slot], lsem.at[slot]) for slot in range(2)]
    for load in loads:
        load.start()
    first = lax.broadcasted_iota(jnp.int32, (512, WIDTH), 1) < SPEC
    scale = 1.0 / math.sqrt(WIDTH)
    stores = []
    for slot in range(2):
        loads[slot].wait()
        ours = held[slot, pl.ds(pl.multiple_of(half, 512), 512), :].astype(jnp.float32)
        rolled = pltpu.roll(ours, SPEC, 1)
        turned[slot] = jnp.where(first, rolled, -rolled).astype(jnp.bfloat16)
        for part in range(2):
            for top in (0, 256):
                rows = pl.ds(top, 256)
                left = turned[slot, rows] if part else held[slot, pl.ds(pl.multiple_of(half + top, 256), 256), :]
                made[slot, part, rows] = (rows_by(left, held[slot]) * scale).astype(jnp.bfloat16)
                stores.append(
                    pltpu.make_async_copy(made.at[slot, part, rows], out.at[slot, part, rows], osem.at[len(stores)]))
                stores[-1].start()
    for store in stores:
        store.wait()


def visibilities(lines):
    return pl.pallas_call(
        visibility_kernel,
        out_shape=jax.ShapeDtypeStruct((2, 2, 512, 1024), jnp.bfloat16),
        in_specs=[pl.BlockSpec(memory_space=pl.ANY)],
        out_specs=pl.BlockSpec(memory_space=pl.ANY),
        scratch_shapes=[
            pltpu.VMEM((2, 1024, WIDTH), jnp.bfloat16),
            pltpu.VMEM((2, 512, WIDTH), jnp.bfloat16),
            pltpu.VMEM((2, 2, 512, 1024), jnp.bfloat16),
            pltpu.SemaphoreType.DMA((2,)),
            pltpu.SemaphoreType.DMA((8,)),
        ],
        compiler_params=pltpu.CompilerParams(vmem_limit_bytes=60 << 20),
        name="visibilities",
    )(lines)


def shards(volts, taps, owner_map, assign):
    blocks = volts.reshape(BATCHES, 2, 2, BLOCKS, 4, 128).transpose(0, 1, 3, 4, 2, 5)
    lines = exchange(
        blocks.reshape(BATCHES, 2, BLOCKS, 8, 128),
        taps,
        owner_map,
        assign.reshape(1, 512),
    )
    return visibilities(lines)


def solution(mesh):
    placed = (P(None, ("chan", "row", "col"), None, None), P(), P(), P())
    return jax.shard_map(
        shards,
        mesh=mesh,
        in_specs=placed,
        out_specs=P(("chan", "col"), None, "row", None),
        check_vma=False,
    )
```
